32 devices in a mesh: dp: 8 (over z, core), mp: 4 (over y, x).
Axes of the slice: x: 2, y: 2, z: 4, core: 2. Of those that a mesh axis runs over, the one named last changes fastest.
Arguments:
- inputs: bfloat16 [8, 48, 48, 3072], P('dp', 'mp'), may hold values from -6 to 6
- cotangent: bfloat16 [8, 48, 48, 3072], P('dp', 'mp'), may hold values from -6 to 6
- mode_weights: bfloat16 [2, 256, 7, 4096], P(None, 'mp'), may hold values from -4.1875 to 4.1875
- local_weight: bfloat16 [64, 64], replicated, may hold values from -0.75 to 0.75
- local_bias: float32 [64], replicated, may hold values from -3 to 3
Outputs:
- outputs: bfloat16 [8, 48, 48, 3072], P('dp', 'mp')
- input_grads: bfloat16 [8, 48, 48, 3072], P('dp', 'mp')
- mode_grads: float32 [2, 256, 7, 4096], P(None, 'mp')
The draws below stay inside these ranges and needn't reach their ends.
All inputs are finite; a program needn't handle non-finite values.
Results may differ from the reference program's by a relative error of at most 0.0012.
Values sent between devices are 32-bit elements; how exact they have to be, the bound alone decides.
A program may use at most 192 MiB of HBM per device.

```python
import functools
import jax
import jax.numpy as jnp
from jax import lax

C = 64
GRID = 48
MX = 8
MZ = 7
SAMPLES = 8
PAIRS = 256


def block_scale(rng, dims, pieces, least, top_value):
    gain = 1.0
    for dim, shards_of in pieces:
        steps = jax.random.uniform(jax.random.fold_in(jax.random.fold_in(rng, 6), dim), (shards_of,), jnp.float32, least / len(pieces), top_value / len(pieces))
        gain = gain * jnp.repeat(jnp.exp(steps), dims[dim] // shards_of).reshape((-1,) + (1,) * (len(dims) - 1 - dim))
    return gain


def gaussian(rng, dims, scale, reach, cuts=(), kind=jnp.bfloat16):
    level = block_scale(rng, dims, cuts, -0.22, 0.18) if cuts else 1.0
    result = jax.random.normal(rng, dims, jnp.float32) * scale * level
    return jnp.minimum(jnp.maximum(result, -reach), reach).astype(kind)


def setup_inputs(seed: int = 0) -> dict:
    keys = jax.random.split(jax.random.key(seed), 6)
    return {
        "inputs": gaussian(keys[0], (SAMPLES, GRID, GRID, GRID * C), 1.0, 6.0, ((0, 8), (1, 4))),
        "cotangent": gaussian(keys[1], (SAMPLES, GRID, GRID, GRID * C), 1.0, 6.0, ((0, 8), (1, 4))),
        "mode_weights": gaussian(keys[2], (2, PAIRS, MZ, C * C), 0.7, 4.1875, ((1, 4),)),
        "local_weight": gaussian(keys[3], (C, C), C ** -0.5, 0.75),
        "local_bias": gaussian(keys[4], (C,), 0.5, 3.0, (), jnp.float32),
    }


highest = lax.Precision.HIGHEST

def kept_freqs():
    lowest = jnp.arange(MX, dtype=jnp.int32)
    return jnp.concatenate([lowest, GRID - MX + lowest]).astype(jnp.int32)

def spectral_part(field, weight_real, weight_imag):
    full = jnp.fft.rfftn(field, axes=(1, 2, 0))
    freqs = kept_freqs()
    modes = full[:MZ][:, freqs][:, :, freqs]
    mode_real = jnp.real(modes)
    mode_imag = jnp.imag(modes)
    mixed_real = jnp.einsum('kabi,abkio->kabo', mode_real, weight_real, precision=highest) - jnp.einsum('kabi,abkio->kabo', mode_imag, weight_imag, precision=highest)
    mixed_imag = jnp.einsum('kabi,abkio->kabo', mode_real, weight_imag, precision=highest) + jnp.einsum('kabi,abkio->kabo', mode_imag, weight_real, precision=highest)
    mixed = mixed_real + 1j * mixed_imag
    zindex = jnp.arange(MZ, dtype=jnp.int32)
    spread = jnp.zeros((GRID // 2 + 1, GRID, GRID, C), dtype=mixed.dtype)
    spread = spread.at[zindex[:, None, None], freqs[None, :, None], freqs[None, None, :]].set(mixed)
    return jnp.fft.irfftn(spread, s=(GRID, GRID, GRID), axes=(1, 2, 0))

def reference(inputs, cotangent, mode_weights, local_weight, local_bias):
    weights = mode_weights.astype(jnp.float32).reshape(2, 2 * MX, 2 * MX, MZ, C, C)
    gelu_fn = functools.partial(jax.nn.gelu, approximate=True)

    def one_sample(carry, pair):
        field, cotan = pair
        field_four = field.reshape(GRID, GRID, GRID, C)
        spectral, pull_back = jax.vjp(spectral_part, field_four.astype(jnp.float32), weights[0], weights[1])
        local = jnp.dot(field.reshape(-1, C), local_weight, preferred_element_type=jnp.float32)
        pre = spectral + local.reshape(spectral.shape) + local_bias
        active, gelu_pull = jax.vjp(gelu_fn, pre)
        slope, = gelu_pull(cotan.reshape(GRID, GRID, GRID, C).astype(jnp.float32))
        field_grad, grad_real, grad_imag = pull_back(slope)
        local_grad = jnp.dot(slope.reshape(-1, C), local_weight.astype(jnp.float32).T, precision=highest)
        total = (field_grad + local_grad.reshape(field_grad.shape)).astype(jnp.bfloat16)
        new_carry = (carry[0] + grad_real, carry[1] + grad_imag)
        return (new_carry, (active.astype(jnp.bfloat16).reshape(GRID, GRID, GRID * C), total.reshape(GRID, GRID, GRID * C)))
    empty = jnp.zeros((2 * MX, 2 * MX, MZ, C, C), jnp.float32)
    sums, stacked = lax.scan(one_sample, (empty, empty), (inputs, cotangent))
    mode_grads = jnp.stack([sums[0], sums[1]]).reshape(2, PAIRS, MZ, C * C)
    return (stacked[0], stacked[1], mode_grads)
```

```python
import functools
import math

import jax
import jax.numpy as jnp
import ml_dtypes
import numpy as np
from jax import lax
from jax.experimental import pallas as pl
from jax.experimental.pallas import tpu as pltpu
from jax.sharding import PartitionSpec as P

MX = 8
LANES = 128
WIDE = 256
ROWS = 8
F32 = jnp.float32
BF16 = jnp.bfloat16
PARAMS = dict(vmem_limit_bytes=50 * 2**20)


def mm(a, b):
    return jnp.dot(a, b, preferred_element_type=F32)


def np_split(table):
    hi = table.astype(ml_dtypes.bfloat16)
    lo = (table - hi.astype(np.float64)).astype(ml_dtypes.bfloat16)
    return hi, lo


def split(x):
    hi = x.astype(BF16).astype(F32)
    return hi, x - hi


def stack_three(x):
    hi, lo = split(x)
    return jnp.concatenate([hi, lo, hi], axis=0).astype(BF16)


def np_three(table):
    hi, lo = np_split(table)
    return np.concatenate([hi, hi, lo], axis=1)


def np_tables(grid, zmodes):
    freqs = np.concatenate([np.arange(MX), grid - MX + np.arange(MX)])
    cells = np.arange(grid)
    ang = 2.0 * math.pi / grid * (freqs[:, None] * cells[None, :] % grid)
    half = 2.0 * math.pi / grid * (freqs[:, None] * (2 * np.arange(grid // 2))[None, :] % grid)
    tw = 2.0 * math.pi / grid * freqs
    count = freqs.size
    fwd_x = np.concatenate([np.cos(ang), -np.sin(ang)], axis=0)
    hi, lo = np_split(fwd_x)
    fwd_x_two = np.concatenate([hi, lo], axis=0)
    fwd_x_three = np_three(fwd_x)
    fwd_y = np_three(np.concatenate([np.cos(half), np.sin(half)], axis=0))
    inv_y = np_three(np.concatenate([np.cos(half.T), np.sin(half.T)], axis=0))
    inv_x = np_three(np.concatenate([np.cos(ang.T), -np.sin(ang.T)], axis=1))
    tw_c = np.ones((count, LANES), np.float32)
    tw_s = np.zeros((count, LANES), np.float32)
    tw_c[:, LANES // 2:] = np.cos(tw)[:, None]
    tw_s[:, LANES // 2:] = np.sin(tw)[:, None]
    kz = np.zeros((ROWS,), np.int64)
    kz[:zmodes] = np.arange(zmodes)
    zang = 2.0 * math.pi / grid * (cells[:, None] * kz[None, :] % grid)
    z_c = np.cos(zang).astype(np.float32)
    z_s = np.sin(zang).astype(np.float32)
    scale = (np.where(kz == 0, 1.0, 2.0) / float(grid**3)).astype(np.float32)
    return dict(fwd_x_two=fwd_x_two, fwd_x_three=fwd_x_three, fwd_y=fwd_y, inv_y=inv_y,
                inv_x=inv_x, tw_c=tw_c, tw_s=tw_s, z_c=z_c, z_s=z_s, scale=scale)


def low_half(shape):
    return lax.broadcasted_iota(jnp.int32, shape, len(shape) - 1) % LANES < LANES // 2


def roll_half(x):
    return pltpu.roll(x, LANES // 2, x.ndim - 1)


def put_rows(g_ref, chunk, first, half):
    for r in range(0, chunk.shape[0], 8):
        for j in range(chunk.shape[1] // LANES):
            g_ref[pl.ds(r * half + first + j, 8, stride=half), :] = chunk[r:r + 8, j * LANES:(j + 1) * LANES]


def get_rows(n_ref, first, blocks, rows, half):
    cols = []
    for j in range(blocks):
        cols.append(jnp.concatenate(
            [n_ref[pl.ds(r * half + first + j, 8, stride=half), :] for r in range(0, rows, 8)], axis=0))
    return jnp.concatenate(cols, axis=1)


def fwd_yz(g_ref, acc_ref, fy, twc, tws, zc_ref, zs_ref, z, zmodes, half):
    count = 2 * MX
    low = low_half((count, LANES))
    sign = jnp.where(low, 1.0, -1.0).astype(F32)
    cs = [zc_ref[z, k] for k in range(zmodes)]
    sn = [zs_ref[z, k] for k in range(zmodes)]
    for a in range(count):
        g = jnp.concatenate([g_ref[a * half:(a + 1) * half, :],
                             g_ref[(count + a) * half:(count + a + 1) * half, :]], axis=1)
        h = mm(fy, stack_three(g))
        re = h[:count, :LANES] + h[count:, LANES:]
        im = h[:count, LANES:] - h[count:, :LANES]
        re2 = re * twc + im * tws
        im2 = im * twc - re * tws
        row = jnp.where(low, re2 + roll_half(re2), im2 + roll_half(im2))
        turned = sign * roll_half(row)
        for k in range(zmodes):
            acc_ref[k, a * count:(a + 1) * count, :] += cs[k] * row + sn[k] * turned


def give_modes(acc_ref, out_ref, zmodes):
    pairs = acc_ref.shape[1]
    for k in range(zmodes):
        out_ref[pl.ds(k, pairs, stride=ROWS), :] = acc_ref[k]
    for k in range(zmodes, ROWS):
        out_ref[pl.ds(k, pairs, stride=ROWS), :] = jnp.zeros((pairs, LANES), F32)


def take_modes(m_ref, scr, zmodes):
    pairs = scr.shape[1]
    for k in range(zmodes):
        scr[k] = m_ref[pl.ds(k, pairs, stride=ROWS), :]


def inv_zy(scr, n_ref, iy, twc, tws, zc_ref, zs_ref, z, zmodes, half):
    count = 2 * MX
    low = low_half((count, LANES))
    sign = jnp.where(low, -1.0, 1.0).astype(F32)
    cs = [zc_ref[z, k] for k in range(zmodes)]
    sn = [zs_ref[z, k] for k in range(zmodes)]
    for a in range(count):
        part = scr[0, a * count:(a + 1) * count, :]
        first, second = cs[0] * part, sn[0] * part
        for k in range(1, zmodes):
            part = scr[k, a * count:(a + 1) * count, :]
            first += cs[k] * part
            second += sn[k] * part
        line = first + sign * roll_half(second)
        other = roll_half(line)
        re = jnp.where(low, line, other)
        im = jnp.where(low, other, line)
        p_re = re * twc - im * tws
        p_im = im * twc + re * tws
        o = mm(iy, stack_three(jnp.concatenate([p_re, p_im], axis=1)))
        n_ref[a * half:(a + 1) * half, :] = o[:half, :LANES] - o[half:, LANES:]
        n_ref[(count + a) * half:(count + a + 1) * half, :] = o[:half, LANES:] + o[half:, :LANES]


def forward_kernel(zmodes, half, zc_ref, zs_ref, x_ref, fx_ref, fy_ref, twc_ref, tws_ref, out_ref, acc_ref, g_ref):
    z = pl.program_id(0)

    @pl.when(z == 0)
    def _():
        acc_ref[...] = jnp.zeros_like(acc_ref)

    rows = 4 * MX
    for n in range(0, x_ref.shape[3], WIDE):
        u = mm(fx_ref[...], x_ref[0, 0, :, n:n + WIDE])
        put_rows(g_ref, u[:rows] + u[rows:], n // LANES, half)
    fwd_yz(g_ref, acc_ref, fy_ref[...], twc_ref[...], tws_ref[...], zc_ref, zs_ref, z, zmodes, half)

    @pl.when(z == pl.num_programs(0) - 1)
    def _():
        give_modes(acc_ref, out_ref, zmodes)


def middle_kernel(zmodes, half, ic_ref, is_ref, fc_ref, fs_ref, m_ref, x_ref, ct_ref, w_ref, b_ref,
                  iy_ref, ix_ref, fx_ref, fy_ref, twc_ref, tws_ref,
                  out_ref, slope_ref, modes_ref, scr, acc_ref, n_ref, g_ref):
    z = pl.program_id(0)

    @pl.when(z == 0)
    def _():
        acc_ref[...] = jnp.zeros_like(acc_ref)
        take_modes(m_ref, scr, zmodes)

    twc, tws = twc_ref[...], tws_ref[...]
    inv_zy(scr, n_ref, iy_ref[...], twc, tws, ic_ref, is_ref, z, zmodes, half)
    rate = math.sqrt(2.0 / math.pi)
    for n in range(0, x_ref.shape[3], WIDE):
        cols = get_rows(n_ref, n // LANES, WIDE // LANES, 4 * MX, half)
        spectral = mm(ix_ref[...], stack_three(cols))
        u = spectral + mm(x_ref[0, 0, :, n:n + WIDE], w_ref[...]) + b_ref[...]
        square = u * u
        t = jnp.tanh(rate * u * (1.0 + 0.044715 * square))
        gate = 0.5 * (1.0 + t)
        out_ref[0, 0, :, n:n + WIDE] = (u * gate).astype(BF16)
        rise = gate + 0.5 * u * (1.0 - t * t) * (rate * (1.0 + 3.0 * 0.044715 * square))
        slope = ct_ref[0, 0, :, n:n + WIDE].astype(F32) * rise
        slope_ref[0, :, n:n + WIDE] = slope
        put_rows(g_ref, mm(fx_ref[...], stack_three(slope)), n // LANES, half)
    fwd_yz(g_ref, acc_ref, fy_ref[...], twc, tws, fc_ref, fs_ref, z, zmodes, half)

    @pl.when(z == pl.num_programs(0) - 1)
    def _():
        give_modes(acc_ref, modes_ref, zmodes)


def final_kernel(zmodes, half, ic_ref, is_ref, m_ref, slope_ref, w_ref, iy_ref, ix_ref, twc_ref, tws_ref,
                 out_ref, scr, n_ref):
    z = pl.program_id(0)

    @pl.when(z == 0)
    def _():
        take_modes(m_ref, scr, zmodes)

    inv_zy(scr, n_ref, iy_ref[...], twc_ref[...], tws_ref[...], ic_ref, is_ref, z, zmodes, half)
    for n in range(0, slope_ref.shape[2], WIDE):
        cols = get_rows(n_ref, n // LANES, WIDE // LANES, 4 * MX, half)
        total = mm(ix_ref[...], stack_three(cols))
        hi, lo = split(slope_ref[0, :, n:n + WIDE])
        total += mm(hi.astype(BF16), w_ref[...]) + mm(lo.astype(BF16), w_ref[...])
        out_ref[0, 0, :, n:n + WIDE] = total.astype(BF16)


def halves(v):
    low = low_half(v.shape)
    other = roll_half(v)
    return jnp.where(low, v, other), jnp.where(low, other, v)


def mix_kernel(zmodes, recv_ref, w_ref, e_ref, spec_ref, out_ref):
    block = spec_ref.shape[0]
    v = recv_ref[0]
    for s in range(1, recv_ref.shape[0]):
        v += recv_ref[s]
    spec_ref[...] = v
    flat = v.reshape(block * ROWS, LANES)
    both = jnp.concatenate(halves(flat), axis=0)
    hi, lo = split(both)
    left = jnp.where(low_half(both.shape), hi, lo).astype(BF16)
    sum_re = jnp.zeros((block, zmodes, WIDE), F32)
    sum_im = jnp.zeros((block, zmodes, WIDE), F32)
    rows = block * ROWS
    for n in range(0, w_ref.shape[3], WIDE):
        x = mm(left, e_ref[:, n:n + WIDE])
        x_re = x[:rows].reshape(block, ROWS, WIDE)[:, :zmodes]
        x_im = x[rows:].reshape(block, ROWS, WIDE)[:, :zmodes]
        w_re = w_ref[0, :, :, n:n + WIDE].astype(F32)
        w_im = w_ref[1, :, :, n:n + WIDE].astype(F32)
        sum_re += x_re * w_re - x_im * w_im
        sum_im += x_re * w_im + x_im * w_re
    half_re = sum_re[..., :LANES] + sum_re[..., LANES:]
    half_im = sum_im[..., :LANES] + sum_im[..., LANES:]
    half_re += roll_half(half_re)
    half_im += roll_half(half_im)
    out_ref[...] = jnp.zeros_like(out_ref)
    out_ref[:, :zmodes, :] = jnp.where(low_half(half_re.shape), half_re, half_im)


def back_kernel(zmodes, recv_ref, w_ref, f_ref, spec_ref, out_ref, p_ref):
    block = spec_ref.shape[0]
    v = recv_ref[0]
    for s in range(1, recv_ref.shape[0]):
        v += recv_ref[s]
    spec_ref[...] = v
    c_re, c_im = halves(v)
    c_re = jnp.concatenate([c_re, c_re], axis=2)[:, :zmodes]
    c_im = jnp.concatenate([c_im, c_im], axis=2)[:, :zmodes]
    p_ref[...] = jnp.zeros_like(p_ref)
    rows = block * ROWS
    total = jnp.zeros((4 * rows, LANES), F32)
    for n in range(0, w_ref.shape[3], WIDE):
        w_re = w_ref[0, :, :, n:n + WIDE].astype(F32)
        w_im = w_ref[1, :, :, n:n + WIDE].astype(F32)
        slot = n // WIDE % 2
        p_ref[slot, 0, :, :zmodes, :] = c_re * w_re + c_im * w_im
        p_ref[slot, 1, :, :zmodes, :] = c_im * w_re - c_re * w_im
        hi, lo = split(p_ref[slot].reshape(2 * rows, WIDE))
        total += mm(jnp.concatenate([hi, lo], axis=0).astype(BF16), f_ref[n:n + WIDE, :])
    total = total[:2 * rows] + total[2 * rows:]
    both = jnp.where(low_half((rows, LANES)), total[:rows], total[rows:])
    out_ref[...] = both.reshape(block, ROWS, LANES)


def grads_kernel(zmodes, samples, stride, v_ref, c_ref, out_ref, x_ref):
    block = out_ref.shape[1]
    chan = LANES // 2
    low = low_half((ROWS, LANES))
    sign = jnp.where(low_half((samples, LANES)), 1.0, -1.0).astype(F32)
    base = pl.program_id(0) * block * ROWS
    for q in range(block):
        slot = q % 2
        for k in range(zmodes):
            at = pl.ds(base + (q * ROWS + k), samples, stride=stride)
            a = v_ref[at, :]
            b = c_ref[at, :]
            left = jnp.concatenate([a, roll_half(a)], axis=0)
            right = jnp.concatenate([b, sign * roll_half(b)], axis=0)
            l_hi, l_lo = split(left)
            r_hi, r_lo = split(right)
            lhs = jnp.concatenate([l_hi, l_lo, l_hi], axis=0).astype(BF16)[:, :chan]
            rhs = jnp.concatenate([r_hi, r_hi, r_lo], axis=0).astype(BF16)
            x_ref[slot, k * chan:(k + 1) * chan, :] = lax.dot_general(
                lhs, rhs, (((0,), (0,)), ((), ())), preferred_element_type=F32)
        for j in range(chan // 2):
            even = x_ref[slot, pl.ds(2 * j, ROWS, stride=chan), :]
            odd = x_ref[slot, pl.ds(2 * j + 1, ROWS, stride=chan), :]
            lanes = slice(j * LANES, (j + 1) * LANES)
            out_ref[0, q, :, lanes] = jnp.where(low, even, roll_half(odd))[:zmodes]
            out_ref[1, q, :, lanes] = jnp.where(low, roll_half(even), odd)[:zmodes]


def whole(a):
    rank = a.ndim
    return pl.BlockSpec(a.shape, lambda i: (0,) * rank)


SMEM = pl.BlockSpec(memory_space=pltpu.SMEM)


def on_device(parts, inputs, cotangent, mode_weights, local_weight, local_bias):
    _, planes, grid, width = inputs.shape
    chan = local_weight.shape[0]
    pairs_here, zmodes, entries = mode_weights.shape[1:]
    pairs = pairs_here * parts
    half = grid // 2
    tab = np_tables(grid, zmodes)
    const = {name: jnp.asarray(t) for name, t in tab.items()}
    first = lax.axis_index("mp") * planes
    z_c = lax.dynamic_slice_in_dim(const["z_c"], first, planes, 0)
    z_s = lax.dynamic_slice_in_dim(const["z_s"], first, planes, 0)
    zsc_c, zsc_s = z_c * const["scale"], z_s * const["scale"]
    params = pltpu.CompilerParams(**PARAMS)
    plane = pl.BlockSpec((1, 1, grid, width), lambda z: (0, z, 0, 0))
    flat = pl.BlockSpec((1, grid, width), lambda z: (z, 0, 0))
    modes_shape = jax.ShapeDtypeStruct((pairs * ROWS, LANES), F32)
    modes_spec = pl.BlockSpec((pairs * ROWS, LANES), lambda z: (0, 0))
    acc = pltpu.VMEM((zmodes, pairs, LANES), F32)
    lines = pltpu.VMEM((4 * MX * half, LANES), F32)
    fy, iy, ix, twc, tws = (const[n] for n in ("fwd_y", "inv_y", "inv_x", "tw_c", "tw_s"))
    fx2, fx3 = const["fwd_x_two"], const["fwd_x_three"]

    def exchange(x):
        return lax.all_to_all(x.reshape(parts, pairs_here, ROWS, LANES), "mp", 0, 0)

    def spread(x):
        every = jnp.broadcast_to(x[None], (parts,) + x.shape)
        return lax.all_to_all(every, "mp", 0, 0).reshape(pairs * ROWS, LANES)

    partial = pl.pallas_call(
        functools.partial(forward_kernel, zmodes, half),
        grid=(planes,),
        in_specs=[SMEM, SMEM, plane, whole(fx2), whole(fy), whole(twc), whole(tws)],
        out_specs=modes_spec, out_shape=modes_shape, scratch_shapes=[acc, lines],
        compiler_params=params, name="forward",
    )(z_c, z_s, inputs, fx2, fy, twc, tws)

    block = 8
    recv_spec = pl.BlockSpec((parts, block, ROWS, LANES), lambda i: (0, i, 0, 0))
    w_spec = pl.BlockSpec((2, block, zmodes, entries), lambda i: (0, i, 0, 0))
    m_spec = pl.BlockSpec((block, ROWS, LANES), lambda i: (i, 0, 0))
    m_shape = jax.ShapeDtypeStruct((pairs_here, ROWS, LANES), F32)
    eye = np.eye(chan, dtype=np.float32)
    expand = np.concatenate([np.repeat(eye, chan, axis=1)] * 2, axis=0)
    fold = np.repeat(np.concatenate([eye, eye], axis=1), chan, axis=0)
    expand, fold = jnp.asarray(expand, BF16), jnp.asarray(fold, BF16)
    spectrum, mixed = pl.pallas_call(
        functools.partial(mix_kernel, zmodes),
        grid=(pairs_here // block,),
        in_specs=[recv_spec, w_spec, whole(expand)],
        out_specs=[m_spec, m_spec], out_shape=[m_shape, m_shape],
        compiler_params=params, name="mix",
    )(exchange(partial), mode_weights, expand)
    all_spectra = lax.all_gather(spectrum, "dp")

    repeat = WIDE // chan
    eyes = jnp.eye(repeat, dtype=BF16)
    w_wide = jnp.kron(eyes, local_weight)
    wt_wide = jnp.kron(eyes, local_weight.T)
    bias = jnp.tile(local_bias, repeat)[None, :]
    outputs, slope, cot_partial = pl.pallas_call(
        functools.partial(middle_kernel, zmodes, half),
        grid=(planes,),
        in_specs=[SMEM] * 4 + [modes_spec, plane, plane, whole(w_wide), whole(bias), whole(iy), whole(ix),
                               whole(fx3), whole(fy), whole(twc), whole(tws)],
        out_specs=[plane, flat, modes_spec],
        out_shape=[jax.ShapeDtypeStruct(inputs.shape, BF16),
                   jax.ShapeDtypeStruct((planes, grid, width), F32), modes_shape],
        scratch_shapes=[acc, acc, lines, lines],
        compiler_params=params, name="middle",
    )(zsc_c, zsc_s, zsc_c, zsc_s, spread(mixed), inputs, cotangent, w_wide, bias, iy, ix, fx3, fy, twc, tws)

    cot_spectrum, back = pl.pallas_call(
        functools.partial(back_kernel, zmodes),
        grid=(pairs_here // block,),
        in_specs=[recv_spec, w_spec, whole(fold)],
        out_specs=[m_spec, m_spec], out_shape=[m_shape, m_shape],
        scratch_shapes=[pltpu.VMEM((2, 2, block, ROWS, WIDE), F32)],
        compiler_params=params, name="back",
    )(exchange(cot_partial), mode_weights, fold)
    all_cots = lax.all_gather(cot_spectrum, "dp")

    input_grads = pl.pallas_call(
        functools.partial(final_kernel, zmodes, half),
        grid=(planes,),
        in_specs=[SMEM] * 2 + [modes_spec, flat, whole(wt_wide), whole(iy), whole(ix), whole(twc), whole(tws)],
        out_specs=plane, out_shape=jax.ShapeDtypeStruct(inputs.shape, BF16),
        scratch_shapes=[acc, lines],
        compiler_params=params, name="final",
    )(z_c, z_s, spread(back), slope, wt_wide, iy, ix, twc, tws)

    samples = all_spectra.shape[0]
    stride = pairs_here * ROWS
    gathered = pl.BlockSpec((samples * stride, LANES), lambda i: (0, 0))
    group = 4
    mode_grads = pl.pallas_call(
        functools.partial(grads_kernel, zmodes, samples, stride),
        grid=(pairs_here // group,),
        in_specs=[gathered, gathered],
        out_specs=pl.BlockSpec((2, group, zmodes, entries), lambda i: (0, i, 0, 0)),
        out_shape=jax.ShapeDtypeStruct((2, pairs_here, zmodes, entries), F32),
        scratch_shapes=[pltpu.VMEM((2, ROWS * chan, LANES), F32)],
        compiler_params=params, name="grads",
    )(all_spectra.reshape(samples * stride, LANES), all_cots.reshape(samples * stride, LANES))
    return (outputs, input_grads, mode_grads)


def solution(mesh):
    field = P("dp", "mp", None, None)
    weights = P(None, "mp", None, None)
    return jax.shard_map(
        functools.partial(on_device, mesh.shape["mp"]),
        mesh=mesh,
        in_specs=(field, field, weights, P(), P()),
        out_specs=(field, field, weights),
        check_vma=False,
    )
```

```python
import functools
import math

import jax
import jax.numpy as jnp
import ml_dtypes
import numpy as np
from jax import lax
from jax.experimental import pallas as pl
from jax.experimental.pallas import tpu as pltpu
from jax.sharding import PartitionSpec as P

MX = 8
LANES = 128
WIDE = 256
F32 = jnp.float32
BF16 = jnp.bfloat16
PARAMS = dict(vmem_limit_bytes=50 * 2**20)


def mm(a, b):
    return jnp.dot(a, b, preferred_element_type=F32)


def np_split(table):
    hi = table.astype(ml_dtypes.bfloat16)
    lo = (table - hi.astype(np.float64)).astype(ml_dtypes.bfloat16)
    return hi, lo


def split(x):
    hi = x.astype(BF16).astype(F32)
    return hi, x - hi


def stack_three(x):
    hi, lo = split(x)
    return jnp.concatenate([hi, lo, hi], axis=0).astype(BF16)


def np_three(table):
    hi, lo = np_split(table)
    return np.concatenate([hi, hi, lo], axis=1)


def np_tables(grid, zmodes):
    freqs = np.concatenate([np.arange(MX), grid - MX + np.arange(MX)])
    cells = np.arange(grid)
    ang = 2.0 * math.pi / grid * (freqs[:, None] * cells[None, :] % grid)
    half = 2.0 * math.pi / grid * (freqs[:, None] * (2 * np.arange(grid // 2))[None, :] % grid)
    tw = 2.0 * math.pi / grid * freqs
    count = freqs.size
    fwd_x = np.concatenate([np.cos(ang), -np.sin(ang)], axis=0)
    hi, lo = np_split(fwd_x)
    fwd_x_two = np.concatenate([hi, lo], axis=0)
    fwd_x_three = np_three(fwd_x)
    fwd_y = np_three(np.concatenate([np.cos(half), np.sin(half)], axis=0))
    inv_y = np_three(np.concatenate([np.cos(half.T), np.sin(half.T)], axis=0))
    inv_x = np_three(np.concatenate([np.cos(ang.T), -np.sin(ang.T)], axis=1))
    tw_c = np.ones((count, LANES), np.float32)
    tw_s = np.zeros((count, LANES), np.float32)
    tw_c[:, LANES // 2:] = np.cos(tw)[:, None]
    tw_s[:, LANES // 2:] = np.sin(tw)[:, None]
    kz = np.arange(zmodes)
    zang = 2.0 * math.pi / grid * (cells[:, None] * kz[None, :] % grid)
    scale = np.where(kz == 0, 1.0, 2.0) / float(grid**3)
    waves = np.stack([np.cos(zang), np.sin(zang)], axis=1)
    z_table = np.concatenate([waves, waves * scale], axis=1).astype(np.float32)
    return dict(fwd_x_two=fwd_x_two, fwd_x_three=fwd_x_three, fwd_y=fwd_y, inv_y=inv_y,
                inv_x=inv_x, tw_c=tw_c, tw_s=tw_s, z_table=z_table)


def low_half(shape):
    return lax.broadcasted_iota(jnp.int32, shape, len(shape) - 1) % LANES < LANES // 2


def roll_half(x):
    return pltpu.roll(x, LANES // 2, x.ndim - 1)


def put_rows(g_ref, chunk, first, half):
    for r in range(0, chunk.shape[0], 8):
        for j in range(chunk.shape[1] // LANES):
            g_ref[pl.ds(r * half + first + j, 8, stride=half), :] = chunk[r:r + 8, j * LANES:(j + 1) * LANES]


def get_rows(n_ref, first, blocks, rows, half):
    cols = []
    for j in range(blocks):
        cols.append(jnp.concatenate(
            [n_ref[pl.ds(r * half + first + j, 8, stride=half), :] for r in range(0, rows, 8)], axis=0))
    return jnp.concatenate(cols, axis=1)


def fwd_yz(g_ref, acc_ref, fy, twc, tws, z_ref, kind, z, zmodes, half):
    count = 2 * MX
    low = low_half((count, LANES))
    sign = jnp.where(low, 1.0, -1.0).astype(F32)
    cs = [z_ref[z, kind * zmodes + k] for k in range(zmodes)]
    sn = [z_ref[z, (kind + 1) * zmodes + k] for k in range(zmodes)]
    for a in range(count):
        g = jnp.concatenate([g_ref[a * half:(a + 1) * half, :],
                             g_ref[(count + a) * half:(count + a + 1) * half, :]], axis=1)
        h = mm(fy, stack_three(g))
        re = h[:count, :LANES] + h[count:, LANES:]
        im = h[:count, LANES:] - h[count:, :LANES]
        re2 = re * twc + im * tws
        im2 = im * twc - re * tws
        row = jnp.where(low, re2 + roll_half(re2), im2 + roll_half(im2))
        turned = sign * roll_half(row)
        for k in range(zmodes):
            acc_ref[k, a * count:(a + 1) * count, :] += cs[k] * row + sn[k] * turned


def give_modes(acc_ref, out_ref, zmodes):
    here = out_ref.shape[2]
    for part in range(out_ref.shape[0]):
        out_ref[part] = acc_ref[:, part * here:(part + 1) * here, :]


def inv_zy(m_ref, n_ref, iy, twc, tws, z_ref, kind, z, zmodes, half):
    count = 2 * MX
    low = low_half((count, LANES))
    sign = jnp.where(low, -1.0, 1.0).astype(F32)
    cs = [z_ref[z, kind * zmodes + k] for k in range(zmodes)]
    sn = [z_ref[z, (kind + 1) * zmodes + k] for k in range(zmodes)]
    share = m_ref.shape[2] // count
    for a in range(count):
        owner, rows = a // share, slice(a % share * count, (a % share + 1) * count)
        part = m_ref[owner, 0, rows, :]
        first, second = cs[0] * part, sn[0] * part
        for k in range(1, zmodes):
            part = m_ref[owner, k, rows, :]
            first += cs[k] * part
            second += sn[k] * part
        line = first + sign * roll_half(second)
        other = roll_half(line)
        re = jnp.where(low, line, other)
        im = jnp.where(low, other, line)
        p_re = re * twc - im * tws
        p_im = im * twc + re * tws
        o = mm(iy, stack_three(jnp.concatenate([p_re, p_im], axis=1)))
        n_ref[a * half:(a + 1) * half, :] = o[:half, :LANES] - o[half:, LANES:]
        n_ref[(count + a) * half:(count + a + 1) * half, :] = o[:half, LANES:] + o[half:, :LANES]


def forward_kernel(zmodes, half, z_ref, x_ref, fx_ref, fy_ref, twc_ref, tws_ref, out_ref, acc_ref, g_ref):
    z = pl.program_id(0)

    @pl.when(z == 0)
    def _():
        acc_ref[...] = jnp.zeros_like(acc_ref)

    rows = 4 * MX
    for n in range(0, x_ref.shape[3], WIDE):
        u = mm(fx_ref[...], x_ref[0, 0, :, n:n + WIDE])
        put_rows(g_ref, u[:rows] + u[rows:], n // LANES, half)
    fwd_yz(g_ref, acc_ref, fy_ref[...], twc_ref[...], tws_ref[...], z_ref, 0, z, zmodes, half)

    @pl.when(z == pl.num_programs(0) - 1)
    def _():
        give_modes(acc_ref, out_ref, zmodes)


def middle_kernel(zmodes, half, z_ref, m_ref, x_ref, ct_ref, w_ref, b_ref,
                  iy_ref, ix_ref, fx_ref, fy_ref, twc_ref, tws_ref,
                  out_ref, slope_ref, modes_ref, acc_ref, n_ref, g_ref):
    z = pl.program_id(0)

    @pl.when(z == 0)
    def _():
        acc_ref[...] = jnp.zeros_like(acc_ref)

    twc, tws = twc_ref[...], tws_ref[...]
    inv_zy(m_ref, n_ref, iy_ref[...], twc, tws, z_ref, 2, z, zmodes, half)
    rate = math.sqrt(2.0 / math.pi)
    for n in range(0, x_ref.shape[3], WIDE):
        cols = get_rows(n_ref, n // LANES, WIDE // LANES, 4 * MX, half)
        spectral = mm(ix_ref[...], stack_three(cols))
        u = spectral + mm(x_ref[0, 0, :, n:n + WIDE], w_ref[...]) + b_ref[...]
        square = u * u
        t = jnp.tanh(rate * u * (1.0 + 0.044715 * square))
        gate = 0.5 * (1.0 + t)
        out_ref[0, 0, :, n:n + WIDE] = (u * gate).astype(BF16)
        rise = gate + 0.5 * u * (1.0 - t * t) * (rate * (1.0 + 3.0 * 0.044715 * square))
        slope = ct_ref[0, 0, :, n:n + WIDE].astype(F32) * rise
        slope_ref[0, :, n:n + WIDE] = slope
        put_rows(g_ref, mm(fx_ref[...], stack_three(slope)), n // LANES, half)
    fwd_yz(g_ref, acc_ref, fy_ref[...], twc, tws, z_ref, 2, z, zmodes, half)

    @pl.when(z == pl.num_programs(0) - 1)
    def _():
        give_modes(acc_ref, modes_ref, zmodes)


def final_kernel(zmodes, half, z_ref, m_ref, slope_ref, w_ref, iy_ref, ix_ref, twc_ref, tws_ref,
                 out_ref, n_ref):
    z = pl.program_id(0)
    inv_zy(m_ref, n_ref, iy_ref[...], twc_ref[...], tws_ref[...], z_ref, 0, z, zmodes, half)
    for n in range(0, slope_ref.shape[2], WIDE):
        cols = get_rows(n_ref, n // LANES, WIDE // LANES, 4 * MX, half)
        total = mm(ix_ref[...], stack_three(cols))
        hi, lo = split(slope_ref[0, :, n:n + WIDE])
        total += mm(hi.astype(BF16), w_ref[...]) + mm(lo.astype(BF16), w_ref[...])
        out_ref[0, 0, :, n:n + WIDE] = total.astype(BF16)


def halves(v):
    low = low_half(v.shape)
    other = roll_half(v)
    return jnp.where(low, v, other), jnp.where(low, other, v)


def mix_kernel(spec_ref, w_ref, e_ref, out_ref):
    zmodes, block, _ = spec_ref.shape
    rows = zmodes * block
    both = jnp.concatenate(halves(spec_ref[...].reshape(rows, LANES)), axis=0)
    hi, lo = split(both)
    left = jnp.where(low_half(both.shape), hi, lo).astype(BF16)
    half_re = jnp.zeros((rows, LANES), F32)
    half_im = jnp.zeros((rows, LANES), F32)
    for n in range(0, w_ref.shape[3], WIDE):
        x = mm(left, e_ref[:, n:n + WIDE])
        x_re, x_im = x[:rows], x[rows:]
        w_re = w_ref[0, :, :, n:n + WIDE].astype(F32).reshape(rows, WIDE)
        w_im = w_ref[1, :, :, n:n + WIDE].astype(F32).reshape(rows, WIDE)
        add_re = x_re * w_re - x_im * w_im
        add_im = x_re * w_im + x_im * w_re
        half_re += add_re[:, :LANES] + add_re[:, LANES:]
        half_im += add_im[:, :LANES] + add_im[:, LANES:]
    half_re += roll_half(half_re)
    half_im += roll_half(half_im)
    mixed = jnp.where(low_half(half_re.shape), half_re, half_im).reshape(spec_ref.shape)
    for part in range(out_ref.shape[0]):
        out_ref[part] = mixed


def back_kernel(spec_ref, w_ref, f_ref, out_ref):
    zmodes, block, _ = spec_ref.shape
    rows = zmodes * block
    c_re, c_im = halves(spec_ref[...].reshape(rows, LANES))
    c_re = jnp.concatenate([c_re, c_re], axis=1)
    c_im = jnp.concatenate([c_im, c_im], axis=1)
    total = jnp.zeros((4 * rows, LANES), F32)
    for n in range(0, w_ref.shape[3], WIDE):
        w_re = w_ref[0, :, :, n:n + WIDE].astype(F32).reshape(rows, WIDE)
        w_im = w_ref[1, :, :, n:n + WIDE].astype(F32).reshape(rows, WIDE)
        both = jnp.concatenate([c_re * w_re + c_im * w_im, c_im * w_re - c_re * w_im], axis=0)
        hi, lo = split(both)
        total += mm(jnp.concatenate([hi, lo], axis=0).astype(BF16), f_ref[n:n + WIDE, :])
    total = total[:2 * rows] + total[2 * rows:]
    both = jnp.where(low_half((rows, LANES)), total[:rows], total[rows:]).reshape(spec_ref.shape)
    for part in range(out_ref.shape[0]):
        out_ref[part] = both


def grads_kernel(samples, pairs, v_ref, c_ref, out_ref, x_ref):
    _, zmodes, block, _ = out_ref.shape
    chan = LANES // 2
    low = low_half((block, LANES))
    sign = jnp.where(low_half((samples, LANES)), 1.0, -1.0).astype(F32)
    base = pl.program_id(0) * block
    for k in range(zmodes):
        slot = k % 2
        for q in range(block):
            at = pl.ds(base + (k * pairs + q), samples, stride=zmodes * pairs)
            a = v_ref[at, :]
            b = c_ref[at, :]
            left = jnp.concatenate([a, roll_half(a)], axis=0)
            right = jnp.concatenate([b, sign * roll_half(b)], axis=0)
            l_hi, l_lo = split(left)
            r_hi, r_lo = split(right)
            lhs = jnp.concatenate([l_hi, l_lo, l_hi], axis=0).astype(BF16)[:, :chan]
            rhs = jnp.concatenate([r_hi, r_hi, r_lo], axis=0).astype(BF16)
            x_ref[slot, q * chan:(q + 1) * chan, :] = lax.dot_general(
                lhs, rhs, (((0,), (0,)), ((), ())), preferred_element_type=F32)
        for j in range(chan // 2):
            even = x_ref[slot, pl.ds(2 * j, block, stride=chan), :]
            odd = x_ref[slot, pl.ds(2 * j + 1, block, stride=chan), :]
            lanes = slice(j * LANES, (j + 1) * LANES)
            out_ref[0, k, :, lanes] = jnp.where(low, even, roll_half(odd))
            out_ref[1, k, :, lanes] = jnp.where(low, roll_half(even), odd)


def whole(a):
    rank = a.ndim
    return pl.BlockSpec(a.shape, lambda i: (0,) * rank)


SMEM = pl.BlockSpec(memory_space=pltpu.SMEM)


def on_device(parts, inputs, cotangent, mode_weights, local_weight, local_bias):
    _, planes, grid, width = inputs.shape
    chan = local_weight.shape[0]
    pairs_here, zmodes, entries = mode_weights.shape[1:]
    pairs = pairs_here * parts
    half = grid // 2
    tab = np_tables(grid, zmodes)
    const = {name: jnp.asarray(t) for name, t in tab.items()}
    z_table = lax.dynamic_slice_in_dim(const["z_table"], lax.axis_index("mp") * planes, planes, 0)
    z_table = z_table.reshape(planes, 4 * zmodes)
    weights = jnp.transpose(mode_weights, (0, 2, 1, 3))
    params = pltpu.CompilerParams(**PARAMS)
    plane = pl.BlockSpec((1, 1, grid, width), lambda z: (0, z, 0, 0))
    flat = pl.BlockSpec((1, grid, width), lambda z: (z, 0, 0))
    modes_shape = jax.ShapeDtypeStruct((parts, zmodes, pairs_here, LANES), F32)
    modes_spec = pl.BlockSpec(modes_shape.shape, lambda z: (0, 0, 0, 0))
    acc = pltpu.VMEM((zmodes, pairs, LANES), F32)
    lines = pltpu.VMEM((4 * MX * half, LANES), F32)
    fy, iy, ix, twc, tws = (const[n] for n in ("fwd_y", "inv_y", "inv_x", "tw_c", "tw_s"))
    fx2, fx3 = const["fwd_x_two"], const["fwd_x_three"]

    def exchange(x):
        return lax.all_to_all(x, "mp", 0, 0)

    partial = pl.pallas_call(
        functools.partial(forward_kernel, zmodes, half),
        grid=(planes,),
        in_specs=[SMEM, plane, whole(fx2), whole(fy), whole(twc), whole(tws)],
        out_specs=modes_spec, out_shape=modes_shape, scratch_shapes=[acc, lines],
        compiler_params=params, name="forward",
    )(z_table, inputs, fx2, fy, twc, tws)

    block = 16
    w_spec = pl.BlockSpec((2, zmodes, block, entries), lambda i: (0, 0, i, 0))
    m_spec = pl.BlockSpec((zmodes, block, LANES), lambda i: (0, i, 0))
    many_spec = pl.BlockSpec((parts, zmodes, block, LANES), lambda i: (0, 0, i, 0))
    eye = np.eye(chan, dtype=np.float32)
    expand = np.concatenate([np.repeat(eye, chan, axis=1)] * 2, axis=0)
    fold = np.repeat(np.concatenate([eye, eye], axis=1), chan, axis=0)
    expand, fold = jnp.asarray(expand, BF16), jnp.asarray(fold, BF16)
    spectrum = jnp.sum(exchange(partial), axis=0)
    all_spectra = lax.all_gather(spectrum, "dp")
    mixed = pl.pallas_call(
        mix_kernel,
        grid=(pairs_here // block,),
        in_specs=[m_spec, w_spec, whole(expand)],
        out_specs=many_spec, out_shape=modes_shape,
        compiler_params=params, name="mix",
    )(spectrum, weights, expand)

    repeat = WIDE // chan
    eyes = jnp.eye(repeat, dtype=BF16)
    w_wide = jnp.kron(eyes, local_weight)
    wt_wide = jnp.kron(eyes, local_weight.T)
    bias = jnp.tile(local_bias, repeat)[None, :]
    outputs, slope, cot_partial = pl.pallas_call(
        functools.partial(middle_kernel, zmodes, half),
        grid=(planes,),
        in_specs=[SMEM, modes_spec, plane, plane, whole(w_wide), whole(bias), whole(iy), whole(ix),
                               whole(fx3), whole(fy), whole(twc), whole(tws)],
        out_specs=[plane, flat, modes_spec],
        out_shape=[jax.ShapeDtypeStruct(inputs.shape, BF16),
                   jax.ShapeDtypeStruct((planes, grid, width), F32), modes_shape],
        scratch_shapes=[acc, lines, lines],
        compiler_params=params, name="middle",
    )(z_table, exchange(mixed), inputs, cotangent, w_wide, bias, iy, ix, fx3, fy, twc, tws)

    cot_spectrum = jnp.sum(exchange(cot_partial), axis=0)
    all_cots = lax.all_gather(cot_spectrum, "dp")
    back = pl.pallas_call(
        back_kernel,
        grid=(pairs_here // block,),
        in_specs=[m_spec, w_spec, whole(fold)],
        out_specs=many_spec, out_shape=modes_shape,
        compiler_params=params, name="back",
    )(cot_spectrum, weights, fold)
    back_lines = exchange(back)

    samples = all_spectra.shape[0]
    rows = samples * zmodes * pairs_here
    gathered = pl.BlockSpec((rows, LANES), lambda i: (0, 0))
    group = 8
    mode_grads = pl.pallas_call(
        functools.partial(grads_kernel, samples, pairs_here),
        grid=(pairs_here // group,),
        in_specs=[gathered, gathered],
        out_specs=pl.BlockSpec((2, zmodes, group, entries), lambda i: (0, 0, i, 0)),
        out_shape=jax.ShapeDtypeStruct((2, zmodes, pairs_here, entries), F32),
        scratch_shapes=[pltpu.VMEM((2, group * chan, LANES), F32)],
        cost_estimate=pl.CostEstimate(flops=2 * 2**30, bytes_accessed=2**26, transcendentals=0),
        compiler_params=params, name="grads",
    )(all_spectra.reshape(rows, LANES), all_cots.reshape(rows, LANES))
    mode_grads, slope = lax.optimization_barrier((mode_grads, slope))
    mode_grads = jnp.transpose(mode_grads, (0, 2, 1, 3))

    input_grads = pl.pallas_call(
        functools.partial(final_kernel, zmodes, half),
        grid=(planes,),
        in_specs=[SMEM, modes_spec, flat, whole(wt_wide), whole(iy), whole(ix), whole(twc), whole(tws)],
        out_specs=plane, out_shape=jax.ShapeDtypeStruct(inputs.shape, BF16),
        scratch_shapes=[lines],
        compiler_params=params, name="final",
    )(z_table, back_lines, slope, wt_wide, iy, ix, twc, tws)
    return (outputs, input_grads, mode_grads)


def solution(mesh):
    field = P("dp", "mp", None, None)
    weights = P(None, "mp", None, None)
    return jax.shard_map(
        functools.partial(on_device, mesh.shape["mp"]),
        mesh=mesh,
        in_specs=(field, field, weights, P(), P()),
        out_specs=(field, field, weights),
        check_vma=False,
    )
```

```python
import functools
import math

import jax
import jax.numpy as jnp
import ml_dtypes
import numpy as np
from jax import lax
from jax.experimental import pallas as pl
from jax.experimental.pallas import tpu as pltpu
from jax.sharding import PartitionSpec as P

MX = 8
LANES = 128
WIDE = 256
F32 = jnp.float32
BF16 = jnp.bfloat16
PARAMS = dict(vmem_limit_bytes=50 * 2**20)


def mm(a, b):
    return jnp.dot(a, b, preferred_element_type=F32)


def np_split(table):
    hi = table.astype(ml_dtypes.bfloat16)
    lo = (table - hi.astype(np.float64)).astype(ml_dtypes.bfloat16)
    return hi, lo


def split(x):
    hi = x.astype(BF16).astype(F32)
    return hi, x - hi


def stack_three(x):
    hi, lo = split(x)
    return jnp.concatenate([hi, lo, hi], axis=0).astype(BF16)


def np_three(table):
    hi, lo = np_split(table)
    return np.concatenate([hi, hi, lo], axis=1)


def np_tables(grid, zmodes):
    freqs = np.concatenate([np.arange(MX), grid - MX + np.arange(MX)])
    cells = np.arange(grid)
    ang = 2.0 * math.pi / grid * (freqs[:, None] * cells[None, :] % grid)
    half = 2.0 * math.pi / grid * (freqs[:, None] * (2 * np.arange(grid // 2))[None, :] % grid)
    tw = 2.0 * math.pi / grid * freqs
    count = freqs.size
    fwd_x = np.concatenate([np.cos(ang), -np.sin(ang)], axis=0)
    hi, lo = np_split(fwd_x)
    fwd_x_two = np.concatenate([hi, lo], axis=0)
    fwd_x_three = np_three(fwd_x)
    fwd_y = np_three(np.concatenate([np.cos(half), np.sin(half)], axis=0))
    inv_y = np_three(np.concatenate([np.cos(half.T), np.sin(half.T)], axis=0))
    inv_x = np_three(np.concatenate([np.cos(ang.T), -np.sin(ang.T)], axis=1))
    tw_c = np.ones((count, LANES), np.float32)
    tw_s = np.zeros((count, LANES), np.float32)
    tw_c[:, LANES // 2:] = np.cos(tw)[:, None]
    tw_s[:, LANES // 2:] = np.sin(tw)[:, None]
    kz = np.arange(zmodes)
    zang = 2.0 * math.pi / grid * (cells[:, None] * kz[None, :] % grid)
    scale = np.where(kz == 0, 1.0, 2.0) / float(grid**3)
    waves = np.stack([np.cos(zang), np.sin(zang)], axis=1)
    z_table = np.concatenate([waves, waves * scale], axis=1).astype(np.float32)
    return dict(fwd_x_two=fwd_x_two, fwd_x_three=fwd_x_three, fwd_y=fwd_y, inv_y=inv_y,
                inv_x=inv_x, tw_c=tw_c, tw_s=tw_s, z_table=z_table)


def low_half(shape):
    return lax.broadcasted_iota(jnp.int32, shape, len(shape) - 1) % LANES < LANES // 2


def roll_half(x):
    return pltpu.roll(x, LANES // 2, x.ndim - 1)


def put_rows(g_ref, chunk, first, half):
    for r in range(0, chunk.shape[0], 8):
        for j in range(chunk.shape[1] // LANES):
            g_ref[pl.ds(r * half + first + j, 8, stride=half), :] = chunk[r:r + 8, j * LANES:(j + 1) * LANES]


def get_rows(n_ref, first, blocks, rows, half):
    cols = []
    for j in range(blocks):
        cols.append(jnp.concatenate(
            [n_ref[pl.ds(r * half + first + j, 8, stride=half), :] for r in range(0, rows, 8)], axis=0))
    return jnp.concatenate(cols, axis=1)


def fwd_yz(g_ref, acc_ref, fy, twc, tws, z_ref, kind, z, zmodes, half):
    count = 2 * MX
    low = low_half((count, LANES))
    sign = jnp.where(low, 1.0, -1.0).astype(F32)
    cs = [z_ref[z, kind * zmodes + k] for k in range(zmodes)]
    sn = [z_ref[z, (kind + 1) * zmodes + k] for k in range(zmodes)]
    for a in range(count):
        g = jnp.concatenate([g_ref[a * half:(a + 1) * half, :],
                             g_ref[(count + a) * half:(count + a + 1) * half, :]], axis=1)
        h = mm(fy, stack_three(g))
        re = h[:count, :LANES] + h[count:, LANES:]
        im = h[:count, LANES:] - h[count:, :LANES]
        re2 = re * twc + im * tws
        im2 = im * twc - re * tws
        row = jnp.where(low, re2 + roll_half(re2), im2 + roll_half(im2))
        turned = sign * roll_half(row)
        for k in range(zmodes):
            acc_ref[k, a * count:(a + 1) * count, :] += cs[k] * row + sn[k] * turned


def give_modes(acc_ref, out_ref, zmodes):
    here = out_ref.shape[2]
    for part in range(out_ref.shape[0]):
        out_ref[part] = acc_ref[:, part * here:(part + 1) * here, :]


def inv_zy(m_ref, n_ref, iy, twc, tws, z_ref, kind, z, zmodes, half):
    count = 2 * MX
    low = low_half((count, LANES))
    sign = jnp.where(low, -1.0, 1.0).astype(F32)
    cs = [z_ref[z, kind * zmodes + k] for k in range(zmodes)]
    sn = [z_ref[z, (kind + 1) * zmodes + k] for k in range(zmodes)]
    share = m_ref.shape[2] // count
    for a in range(count):
        owner, rows = a // share, slice(a % share * count, (a % share + 1) * count)
        part = m_ref[owner, 0, rows, :]
        first, second = cs[0] * part, sn[0] * part
        for k in range(1, zmodes):
            part = m_ref[owner, k, rows, :]
            first += cs[k] * part
            second += sn[k] * part
        line = first + sign * roll_half(second)
        other = roll_half(line)
        re = jnp.where(low, line, other)
        im = jnp.where(low, other, line)
        p_re = re * twc - im * tws
        p_im = im * twc + re * tws
        o = mm(iy, stack_three(jnp.concatenate([p_re, p_im], axis=1)))
        n_ref[a * half:(a + 1) * half, :] = o[:half, :LANES] - o[half:, LANES:]
        n_ref[(count + a) * half:(count + a + 1) * half, :] = o[:half, LANES:] + o[half:, :LANES]


def forward_kernel(zmodes, half, z_ref, x_ref, fx_ref, fy_ref, twc_ref, tws_ref, out_ref, acc_ref, g_ref):
    z = pl.program_id(0)

    @pl.when(z == 0)
    def _():
        acc_ref[...] = jnp.zeros_like(acc_ref)

    rows = 4 * MX
    for n in range(0, x_ref.shape[3], WIDE):
        u = mm(fx_ref[...], x_ref[0, 0, :, n:n + WIDE])
        put_rows(g_ref, u[:rows] + u[rows:], n // LANES, half)
    fwd_yz(g_ref, acc_ref, fy_ref[...], twc_ref[...], tws_ref[...], z_ref, 0, z, zmodes, half)

    @pl.when(z == pl.num_programs(0) - 1)
    def _():
        give_modes(acc_ref, out_ref, zmodes)


def middle_kernel(zmodes, half, z_ref, m_ref, x_ref, ct_ref, w_ref, b_ref,
                  iy_ref, ix_ref, fx_ref, fy_ref, twc_ref, tws_ref,
                  out_ref, slope_ref, modes_ref, acc_ref, n_ref, g_ref, loc_ref):
    z = pl.program_id(0)

    @pl.when(z == 0)
    def _():
        acc_ref[...] = jnp.zeros_like(acc_ref)

    twc, tws = twc_ref[...], tws_ref[...]
    inv_zy(m_ref, n_ref, iy_ref[...], twc, tws, z_ref, 2, z, zmodes, half)
    rate = math.sqrt(2.0 / math.pi)
    width, tall = x_ref.shape[3], x_ref.shape[2]
    loc_ref[...] = mm(jnp.concatenate([x_ref[0, 0, :, n:n + WIDE] for n in range(0, width, WIDE)], axis=0), w_ref[...])
    for n in range(0, x_ref.shape[3], WIDE):
        cols = get_rows(n_ref, n // LANES, WIDE // LANES, 4 * MX, half)
        spectral = mm(ix_ref[...], stack_three(cols))
        at = n // WIDE * tall
        u = spectral + loc_ref[at:at + tall, :] + b_ref[...]
        square = u * u
        t = jnp.tanh(rate * u * (1.0 + 0.044715 * square))
        gate = 0.5 * (1.0 + t)
        out_ref[0, 0, :, n:n + WIDE] = (u * gate).astype(BF16)
        rise = gate + 0.5 * u * (1.0 - t * t) * (rate * (1.0 + 3.0 * 0.044715 * square))
        slope = ct_ref[0, 0, :, n:n + WIDE].astype(F32) * rise
        slope_ref[0, :, n:n + WIDE] = slope
        put_rows(g_ref, mm(fx_ref[...], stack_three(slope)), n // LANES, half)
    fwd_yz(g_ref, acc_ref, fy_ref[...], twc, tws, z_ref, 2, z, zmodes, half)

    @pl.when(z == pl.num_programs(0) - 1)
    def _():
        give_modes(acc_ref, modes_ref, zmodes)


def final_kernel(zmodes, half, z_ref, m_ref, slope_ref, w_ref, iy_ref, ix_ref, twc_ref, tws_ref,
                 out_ref, n_ref, loc_ref):
    z = pl.program_id(0)
    inv_zy(m_ref, n_ref, iy_ref[...], twc_ref[...], tws_ref[...], z_ref, 0, z, zmodes, half)
    width, tall = slope_ref.shape[2], slope_ref.shape[1]
    pieces = [split(slope_ref[0, :, n:n + WIDE]) for n in range(0, width, WIDE)]
    pieces = [piece[part].astype(BF16) for part in range(2) for piece in pieces]
    loc_ref[...] = mm(jnp.concatenate(pieces, axis=0), w_ref[...])
    below = width // WIDE * tall
    for n in range(0, width, WIDE):
        cols = get_rows(n_ref, n // LANES, WIDE // LANES, 4 * MX, half)
        total = mm(ix_ref[...], stack_three(cols))
        at = n // WIDE * tall
        total += loc_ref[at:at + tall, :] + loc_ref[below + at:below + at + tall, :]
        out_ref[0, 0, :, n:n + WIDE] = total.astype(BF16)


def halves(v):
    low = low_half(v.shape)
    other = roll_half(v)
    return jnp.where(low, v, other), jnp.where(low, other, v)


def mix_kernel(spec_ref, w_ref, e_ref, out_ref):
    zmodes, block, _ = spec_ref.shape
    rows = zmodes * block
    both = jnp.concatenate(halves(spec_ref[...].reshape(rows, LANES)), axis=0)
    hi, lo = split(both)
    left = jnp.where(low_half(both.shape), hi, lo).astype(BF16)
    half_re = jnp.zeros((rows, LANES), F32)
    half_im = jnp.zeros((rows, LANES), F32)
    for n in range(0, w_ref.shape[3], WIDE):
        x = mm(left, e_ref[:, n:n + WIDE])
        x_re, x_im = x[:rows], x[rows:]
        w_re = w_ref[0, :, :, n:n + WIDE].astype(F32).reshape(rows, WIDE)
        w_im = w_ref[1, :, :, n:n + WIDE].astype(F32).reshape(rows, WIDE)
        add_re = x_re * w_re - x_im * w_im
        add_im = x_re * w_im + x_im * w_re
        half_re += add_re[:, :LANES] + add_re[:, LANES:]
        half_im += add_im[:, :LANES] + add_im[:, LANES:]
    half_re += roll_half(half_re)
    half_im += roll_half(half_im)
    mixed = jnp.where(low_half(half_re.shape), half_re, half_im).reshape(spec_ref.shape)
    for part in range(out_ref.shape[0]):
        out_ref[part] = mixed


def back_kernel(spec_ref, w_ref, f_ref, out_ref):
    zmodes, block, _ = spec_ref.shape
    rows = zmodes * block
    c_re, c_im = halves(spec_ref[...].reshape(rows, LANES))
    c_re = jnp.concatenate([c_re, c_re], axis=1)
    c_im = jnp.concatenate([c_im, c_im], axis=1)
    total = jnp.zeros((4 * rows, LANES), F32)
    for n in range(0, w_ref.shape[3], WIDE):
        w_re = w_ref[0, :, :, n:n + WIDE].astype(F32).reshape(rows, WIDE)
        w_im = w_ref[1, :, :, n:n + WIDE].astype(F32).reshape(rows, WIDE)
        both = jnp.concatenate([c_re * w_re + c_im * w_im, c_im * w_re - c_re * w_im], axis=0)
        hi, lo = split(both)
        total += mm(jnp.concatenate([hi, lo], axis=0).astype(BF16), f_ref[n:n + WIDE, :])
    total = total[:2 * rows] + total[2 * rows:]
    both = jnp.where(low_half((rows, LANES)), total[:rows], total[rows:]).reshape(spec_ref.shape)
    for part in range(out_ref.shape[0]):
        out_ref[part] = both


def grads_kernel(samples, pairs, v_ref, c_ref, out_ref, x_ref):
    _, zmodes, block, _ = out_ref.shape
    chan = LANES // 2
    low = low_half((block, LANES))
    sign = jnp.where(low_half((samples, LANES)), 1.0, -1.0).astype(F32)
    base = pl.program_id(0) * block
    for k in range(zmodes):
        slot = k % 2
        for q in range(block):
            at = pl.ds(base + (k * pairs + q), samples, stride=zmodes * pairs)
            a = v_ref[at, :]
            b = c_ref[at, :]
            left = jnp.concatenate([a, roll_half(a)], axis=0)
            right = jnp.concatenate([b, sign * roll_half(b)], axis=0)
            l_hi, l_lo = split(left)
            r_hi, r_lo = split(right)
            lhs = jnp.concatenate([l_hi, l_lo, l_hi], axis=0).astype(BF16)[:, :chan]
            rhs = jnp.concatenate([r_hi, r_hi, r_lo], axis=0).astype(BF16)
            x_ref[slot, q * chan:(q + 1) * chan, :] = lax.dot_general(
                lhs, rhs, (((0,), (0,)), ((), ())), preferred_element_type=F32)
        for j in range(chan // 2):
            even = x_ref[slot, pl.ds(2 * j, block, stride=chan), :]
            odd = x_ref[slot, pl.ds(2 * j + 1, block, stride=chan), :]
            lanes = slice(j * LANES, (j + 1) * LANES)
            out_ref[0, k, :, lanes] = jnp.where(low, even, roll_half(odd))
            out_ref[1, k, :, lanes] = jnp.where(low, roll_half(even), odd)


def whole(a):
    rank = a.ndim
    return pl.BlockSpec(a.shape, lambda i: (0,) * rank)


SMEM = pl.BlockSpec(memory_space=pltpu.SMEM)


def on_device(parts, inputs, cotangent, mode_weights, local_weight, local_bias):
    _, planes, grid, width = inputs.shape
    chan = local_weight.shape[0]
    pairs_here, zmodes, entries = mode_weights.shape[1:]
    pairs = pairs_here * parts
    half = grid // 2
    tab = np_tables(grid, zmodes)
    const = {name: jnp.asarray(t) for name, t in tab.items()}
    z_table = lax.dynamic_slice_in_dim(const["z_table"], lax.axis_index("mp") * planes, planes, 0)
    z_table = z_table.reshape(planes, 4 * zmodes)
    weights = jnp.transpose(mode_weights, (0, 2, 1, 3))
    params = pltpu.CompilerParams(**PARAMS)
    plane = pl.BlockSpec((1, 1, grid, width), lambda z: (0, z, 0, 0))
    flat = pl.BlockSpec((1, grid, width), lambda z: (z, 0, 0))
    modes_shape = jax.ShapeDtypeStruct((parts, zmodes, pairs_here, LANES), F32)
    modes_spec = pl.BlockSpec(modes_shape.shape, lambda z: (0, 0, 0, 0))
    acc = pltpu.VMEM((zmodes, pairs, LANES), F32)
    lines = pltpu.VMEM((4 * MX * half, LANES), F32)
    fy, iy, ix, twc, tws = (const[n] for n in ("fwd_y", "inv_y", "inv_x", "tw_c", "tw_s"))
    fx2, fx3 = const["fwd_x_two"], const["fwd_x_three"]

    def exchange(x):
        return lax.all_to_all(x, "mp", 0, 0)

    partial = pl.pallas_call(
        functools.partial(forward_kernel, zmodes, half),
        grid=(planes,),
        in_specs=[SMEM, plane, whole(fx2), whole(fy), whole(twc), whole(tws)],
        out_specs=modes_spec, out_shape=modes_shape, scratch_shapes=[acc, lines],
        compiler_params=params, name="forward",
    )(z_table, inputs, fx2, fy, twc, tws)

    block = 16
    w_spec = pl.BlockSpec((2, zmodes, block, entries), lambda i: (0, 0, i, 0))
    m_spec = pl.BlockSpec((zmodes, block, LANES), lambda i: (0, i, 0))
    many_spec = pl.BlockSpec((parts, zmodes, block, LANES), lambda i: (0, 0, i, 0))
    eye = np.eye(chan, dtype=np.float32)
    expand = np.concatenate([np.repeat(eye, chan, axis=1)] * 2, axis=0)
    fold = np.repeat(np.concatenate([eye, eye], axis=1), chan, axis=0)
    expand, fold = jnp.asarray(expand, BF16), jnp.asarray(fold, BF16)
    spectrum = jnp.sum(exchange(partial), axis=0)
    all_spectra = lax.all_gather(spectrum, "dp")
    mixed = pl.pallas_call(
        mix_kernel,
        grid=(pairs_here // block,),
        in_specs=[m_spec, w_spec, whole(expand)],
        out_specs=many_spec, out_shape=modes_shape,
        compiler_params=params, name="mix",
    )(spectrum, weights, expand)

    repeat = WIDE // chan
    eyes = jnp.eye(repeat, dtype=BF16)
    w_wide = jnp.kron(eyes, local_weight)
    wt_wide = jnp.kron(eyes, local_weight.T)
    bias = jnp.tile(local_bias, repeat)[None, :]
    outputs, slope, cot_partial = pl.pallas_call(
        functools.partial(middle_kernel, zmodes, half),
        grid=(planes,),
        in_specs=[SMEM, modes_spec, plane, plane, whole(w_wide), whole(bias), whole(iy), whole(ix),
                               whole(fx3), whole(fy), whole(twc), whole(tws)],
        out_specs=[plane, flat, modes_spec],
        out_shape=[jax.ShapeDtypeStruct(inputs.shape, BF16),
                   jax.ShapeDtypeStruct((planes, grid, width), F32), modes_shape],
        scratch_shapes=[acc, lines, lines, pltpu.VMEM((width // WIDE * grid, WIDE), F32)],
        compiler_params=params, name="middle",
    )(z_table, exchange(mixed), inputs, cotangent, w_wide, bias, iy, ix, fx3, fy, twc, tws)

    cot_spectrum = jnp.sum(exchange(cot_partial), axis=0)
    all_cots = lax.all_gather(cot_spectrum, "dp")
    back = pl.pallas_call(
        back_kernel,
        grid=(pairs_here // block,),
        in_specs=[m_spec, w_spec, whole(fold)],
        out_specs=many_spec, out_shape=modes_shape,
        compiler_params=params, name="back",
    )(cot_spectrum, weights, fold)
    back_lines = exchange(back)

    input_grads = pl.pallas_call(
        functools.partial(final_kernel, zmodes, half),
        grid=(planes,),
        in_specs=[SMEM, modes_spec, flat, whole(wt_wide), whole(iy), whole(ix), whole(twc), whole(tws)],
        out_specs=plane, out_shape=jax.ShapeDtypeStruct(inputs.shape, BF16),
        scratch_shapes=[lines, pltpu.VMEM((2 * (width // WIDE) * grid, WIDE), F32)],
        compiler_params=params, name="final",
    )(z_table, back_lines, slope, wt_wide, iy, ix, twc, tws)

    all_cots, input_grads = lax.optimization_barrier((all_cots, input_grads))
    samples = all_spectra.shape[0]
    rows = samples * zmodes * pairs_here
    gathered = pl.BlockSpec((rows, LANES), lambda i: (0, 0))
    group = 8
    mode_grads = pl.pallas_call(
        functools.partial(grads_kernel, samples, pairs_here),
        grid=(pairs_here // group,),
        in_specs=[gathered, gathered],
        out_specs=pl.BlockSpec((2, zmodes, group, entries), lambda i: (0, 0, i, 0)),
        out_shape=jax.ShapeDtypeStruct((2, zmodes, pairs_here, entries), F32),
        scratch_shapes=[pltpu.VMEM((2, group * chan, LANES), F32)],
        cost_estimate=pl.CostEstimate(flops=2 * 2**30, bytes_accessed=2**26, transcendentals=0),
        compiler_params=params, name="grads",
    )(all_spectra.reshape(rows, LANES), all_cots.reshape(rows, LANES))
    mode_grads = jnp.transpose(mode_grads, (0, 2, 1, 3))
    return (outputs, input_grads, mode_grads)


def solution(mesh):
    field = P("dp", "mp", None, None)
    weights = P(None, "mp", None, None)
    return jax.shard_map(
        functools.partial(on_device, mesh.shape["mp"]),
        mesh=mesh,
        in_specs=(field, field, weights, P(), P()),
        out_specs=(field, field, weights),
        check_vma=False,
    )
```

```python
import functools
import math

import jax
import jax.numpy as jnp
import ml_dtypes
import numpy as np
from jax import lax
from jax.experimental import pallas as pl
from jax.experimental.pallas import tpu as pltpu
from jax.sharding import PartitionSpec as P

MX = 8
LANES = 128
WIDE = 256
F32 = jnp.float32
BF16 = jnp.bfloat16
PARAMS = dict(vmem_limit_bytes=50 * 2**20)


def mm(a, b):
    return jnp.dot(a, b, preferred_element_type=F32)


def np_split(table):
    hi = table.astype(ml_dtypes.bfloat16)
    lo = (table - hi.astype(np.float64)).astype(ml_dtypes.bfloat16)
    return hi, lo


def split(x):
    hi = x.astype(BF16).astype(F32)
    return hi, x - hi


def stack_three(x):
    hi, lo = split(x)
    return jnp.concatenate([hi, lo, hi], axis=0).astype(BF16)


def np_three(table):
    hi, lo = np_split(table)
    return np.concatenate([hi, hi, lo], axis=1)


def np_tables(grid, zmodes):
    freqs = np.concatenate([np.arange(MX), grid - MX + np.arange(MX)])
    cells = np.arange(grid)
    ang = 2.0 * math.pi / grid * (freqs[:, None] * cells[None, :] % grid)
    half = 2.0 * math.pi / grid * (freqs[:, None] * (2 * np.arange(grid // 2))[None, :] % grid)
    tw = 2.0 * math.pi / grid * freqs
    count = freqs.size
    fwd_x = np.concatenate([np.cos(ang), -np.sin(ang)], axis=0)
    hi, lo = np_split(fwd_x)
    fwd_x_two = np.concatenate([hi, lo], axis=0)
    fwd_x_three = np_three(fwd_x)
    fwd_y = np_three(np.concatenate([np.cos(half), np.sin(half)], axis=0))
    inv_y = np_three(np.concatenate([np.cos(half.T), np.sin(half.T)], axis=0))
    inv_x = np_three(np.concatenate([np.cos(ang.T), -np.sin(ang.T)], axis=1))
    tw_c = np.ones((count, LANES), np.float32)
    tw_s = np.zeros((count, LANES), np.float32)
    tw_c[:, LANES // 2:] = np.cos(tw)[:, None]
    tw_s[:, LANES // 2:] = np.sin(tw)[:, None]
    kz = np.arange(zmodes)
    zang = 2.0 * math.pi / grid * (cells[:, None] * kz[None, :] % grid)
    scale = np.where(kz == 0, 1.0, 2.0) / float(grid**3)
    waves = np.stack([np.cos(zang), np.sin(zang)], axis=1)
    z_table = np.concatenate([waves, waves * scale], axis=1).astype(np.float32)
    return dict(fwd_x_two=fwd_x_two, fwd_x_three=fwd_x_three, fwd_y=fwd_y, inv_y=inv_y,
                inv_x=inv_x, tw_c=tw_c, tw_s=tw_s, z_table=z_table)


def low_half(shape):
    return lax.broadcasted_iota(jnp.int32, shape, len(shape) - 1) % LANES < LANES // 2


def roll_half(x):
    return pltpu.roll(x, LANES // 2, x.ndim - 1)


def put_rows(g_ref, chunk, first, half):
    for r in range(0, chunk.shape[0], 8):
        for j in range(chunk.shape[1] // LANES):
            g_ref[pl.ds(r * half + first + j, 8, stride=half), :] = chunk[r:r + 8, j * LANES:(j + 1) * LANES]


def get_rows(n_ref, first, blocks, rows, half):
    cols = []
    for j in range(blocks):
        cols.append(jnp.concatenate(
            [n_ref[pl.ds(r * half + first + j, 8, stride=half), :] for r in range(0, rows, 8)], axis=0))
    return jnp.concatenate(cols, axis=1)


def fwd_yz(g_ref, acc_ref, fy, twc, tws, z_ref, kind, z, zmodes, half):
    count = 2 * MX
    low = low_half((count, LANES))
    sign = jnp.where(low, 1.0, -1.0).astype(F32)
    cs = [z_ref[z, kind * zmodes + k] for k in range(zmodes)]
    sn = [z_ref[z, (kind + 1) * zmodes + k] for k in range(zmodes)]
    for a in range(count):
        g = jnp.concatenate([g_ref[a * half:(a + 1) * half, :],
                             g_ref[(count + a) * half:(count + a + 1) * half, :]], axis=1)
        h = mm(fy, stack_three(g))
        re = h[:count, :LANES] + h[count:, LANES:]
        im = h[:count, LANES:] - h[count:, :LANES]
        re2 = re * twc + im * tws
        im2 = im * twc - re * tws
        row = jnp.where(low, re2 + roll_half(re2), im2 + roll_half(im2))
        turned = sign * roll_half(row)
        for k in range(zmodes):
            acc_ref[k, a * count:(a + 1) * count, :] += cs[k] * row + sn[k] * turned


def give_modes(acc_ref, out_ref, zmodes):
    here = out_ref.shape[2]
    for part in range(out_ref.shape[0]):
        out_ref[part] = acc_ref[:, part * here:(part + 1) * here, :]


def inv_zy(m_ref, n_ref, iy, twc, tws, z_ref, kind, z, zmodes, half):
    count = 2 * MX
    low = low_half((count, LANES))
    sign = jnp.where(low, -1.0, 1.0).astype(F32)
    cs = [z_ref[z, kind * zmodes + k] for k in range(zmodes)]
    sn = [z_ref[z, (kind + 1) * zmodes + k] for k in range(zmodes)]
    share = m_ref.shape[2] // count
    for a in range(count):
        owner, rows = a // share, slice(a % share * count, (a % share + 1) * count)
        part = m_ref[owner, 0, rows, :]
        first, second = cs[0] * part, sn[0] * part
        for k in range(1, zmodes):
            part = m_ref[owner, k, rows, :]
            first += cs[k] * part
            second += sn[k] * part
        line = first + sign * roll_half(second)
        other = roll_half(line)
        re = jnp.where(low, line, other)
        im = jnp.where(low, other, line)
        p_re = re * twc - im * tws
        p_im = im * twc + re * tws
        o = mm(iy, stack_three(jnp.concatenate([p_re, p_im], axis=1)))
        n_ref[a * half:(a + 1) * half, :] = o[:half, :LANES] - o[half:, LANES:]
        n_ref[(count + a) * half:(count + a + 1) * half, :] = o[:half, LANES:] + o[half:, :LANES]


def forward_kernel(zmodes, half, z_ref, x_ref, fx_ref, fy_ref, twc_ref, tws_ref, out_ref, acc_ref, g_ref):
    z = pl.program_id(0)

    @pl.when(z == 0)
    def _():
        acc_ref[...] = jnp.zeros_like(acc_ref)

    rows = 4 * MX
    for n in range(0, x_ref.shape[3], WIDE):
        u = mm(fx_ref[...], x_ref[0, 0, :, n:n + WIDE])
        put_rows(g_ref, u[:rows] + u[rows:], n // LANES, half)
    fwd_yz(g_ref, acc_ref, fy_ref[...], twc_ref[...], tws_ref[...], z_ref, 0, z, zmodes, half)

    @pl.when(z == pl.num_programs(0) - 1)
    def _():
        give_modes(acc_ref, out_ref, zmodes)


def middle_kernel(zmodes, half, z_ref, m_ref, x_ref, ct_ref, w_ref, b_ref,
                  iy_ref, ix_ref, fx_ref, fy_ref, twc_ref, tws_ref,
                  out_ref, slope_ref, modes_ref, acc_ref, n_ref, g_ref, loc_ref):
    z = pl.program_id(0)

    @pl.when(z == 0)
    def _():
        acc_ref[...] = jnp.zeros_like(acc_ref)

    twc, tws = twc_ref[...], tws_ref[...]
    inv_zy(m_ref, n_ref, iy_ref[...], twc, tws, z_ref, 2, z, zmodes, half)
    rate = math.sqrt(2.0 / math.pi)
    width, tall = x_ref.shape[3], x_ref.shape[2]
    loc_ref[...] = mm(jnp.concatenate([x_ref[0, 0, :, n:n + WIDE] for n in range(0, width, WIDE)], axis=0), w_ref[...])
    for n in range(0, x_ref.shape[3], WIDE):
        cols = get_rows(n_ref, n // LANES, WIDE // LANES, 4 * MX, half)
        spectral = mm(ix_ref[...], stack_three(cols))
        at = n // WIDE * tall
        u = spectral + loc_ref[at:at + tall, :] + b_ref[...]
        square = u * u
        t = jnp.tanh(rate * u * (1.0 + 0.044715 * square))
        gate = 0.5 * (1.0 + t)
        out_ref[0, 0, :, n:n + WIDE] = (u * gate).astype(BF16)
        rise = gate + 0.5 * u * (1.0 - t * t) * (rate * (1.0 + 3.0 * 0.044715 * square))
        slope = ct_ref[0, 0, :, n:n + WIDE].astype(F32) * rise
        slope_ref[0, :, n:n + WIDE] = slope
        put_rows(g_ref, mm(fx_ref[...], stack_three(slope)), n // LANES, half)
    fwd_yz(g_ref, acc_ref, fy_ref[...], twc, tws, z_ref, 2, z, zmodes, half)

    @pl.when(z == pl.num_programs(0) - 1)
    def _():
        give_modes(acc_ref, modes_ref, zmodes)


def final_kernel(zmodes, half, z_ref, m_ref, slope_ref, w_ref, iy_ref, ix_ref, twc_ref, tws_ref,
                 out_ref, n_ref, loc_ref):
    z = pl.program_id(0)
    inv_zy(m_ref, n_ref, iy_ref[...], twc_ref[...], tws_ref[...], z_ref, 0, z, zmodes, half)
    width, tall = slope_ref.shape[2], slope_ref.shape[1]
    pieces = [split(slope_ref[0, :, n:n + WIDE]) for n in range(0, width, WIDE)]
    pieces = [piece[part].astype(BF16) for part in range(2) for piece in pieces]
    loc_ref[...] = mm(jnp.concatenate(pieces, axis=0), w_ref[...])
    below = width // WIDE * tall
    for n in range(0, width, WIDE):
        cols = get_rows(n_ref, n // LANES, WIDE // LANES, 4 * MX, half)
        total = mm(ix_ref[...], stack_three(cols))
        at = n // WIDE * tall
        total += loc_ref[at:at + tall, :] + loc_ref[below + at:below + at + tall, :]
        out_ref[0, 0, :, n:n + WIDE] = total.astype(BF16)


def halves(v):
    low = low_half(v.shape)
    other = roll_half(v)
    return jnp.where(low, v, other), jnp.where(low, other, v)


def mix_kernel(spec_ref, w_ref, e_ref, out_ref):
    zmodes, block, _ = spec_ref.shape
    rows = zmodes * block
    both = jnp.concatenate(halves(spec_ref[...].reshape(rows, LANES)), axis=0)
    hi, lo = split(both)
    left = jnp.where(low_half(both.shape), hi, lo).astype(BF16)
    half_re = jnp.zeros((rows, LANES), F32)
    half_im = jnp.zeros((rows, LANES), F32)
    for n in range(0, w_ref.shape[3], WIDE):
        x = mm(left, e_ref[:, n:n + WIDE])
        x_re, x_im = x[:rows], x[rows:]
        w_re = w_ref[0, :, :, n:n + WIDE].astype(F32).reshape(rows, WIDE)
        w_im = w_ref[1, :, :, n:n + WIDE].astype(F32).reshape(rows, WIDE)
        add_re = x_re * w_re - x_im * w_im
        add_im = x_re * w_im + x_im * w_re
        half_re += add_re[:, :LANES] + add_re[:, LANES:]
        half_im += add_im[:, :LANES] + add_im[:, LANES:]
    half_re += roll_half(half_re)
    half_im += roll_half(half_im)
    mixed = jnp.where(low_half(half_re.shape), half_re, half_im).reshape(spec_ref.shape)
    for part in range(out_ref.shape[0]):
        out_ref[part] = mixed


def back_kernel(spec_ref, w_ref, f_ref, out_ref):
    zmodes, block, _ = spec_ref.shape
    rows = zmodes * block
    c_re, c_im = halves(spec_ref[...].reshape(rows, LANES))
    c_re = jnp.concatenate([c_re, c_re], axis=1)
    c_im = jnp.concatenate([c_im, c_im], axis=1)
    total = jnp.zeros((4 * rows, LANES), F32)
    for n in range(0, w_ref.shape[3], WIDE):
        w_re = w_ref[0, :, :, n:n + WIDE].astype(F32).reshape(rows, WIDE)
        w_im = w_ref[1, :, :, n:n + WIDE].astype(F32).reshape(rows, WIDE)
        both = jnp.concatenate([c_re * w_re + c_im * w_im, c_im * w_re - c_re * w_im], axis=0)
        hi, lo = split(both)
        total += mm(jnp.concatenate([hi, lo], axis=0).astype(BF16), f_ref[n:n + WIDE, :])
    total = total[:2 * rows] + total[2 * rows:]
    both = jnp.where(low_half((rows, LANES)), total[:rows], total[rows:]).reshape(spec_ref.shape)
    for part in range(out_ref.shape[0]):
        out_ref[part] = both


def grads_kernel(samples, pairs, v_ref, c_ref, out_ref, x_ref):
    _, zmodes, block, _ = out_ref.shape
    chan = LANES // 2
    low = low_half((block, LANES))
    sign = jnp.where(low_half((samples, LANES)), 1.0, -1.0).astype(F32)
    base = pl.program_id(0) * block
    for k in range(zmodes):
        slot = k % 2
        for q in range(0, block, 2):
            sides = []
            for pair in (q, q + 1):
                at = pl.ds(base + (k * pairs + pair), samples, stride=zmodes * pairs)
                a = v_ref[at, :]
                b = c_ref[at, :]
                l_hi, l_lo = split(jnp.concatenate([a, roll_half(a)], axis=0))
                r_hi, r_lo = split(jnp.concatenate([b, sign * roll_half(b)], axis=0))
                sides.append((jnp.concatenate([l_hi, l_lo, l_hi], axis=0).astype(BF16),
                              jnp.concatenate([r_hi, r_hi, r_lo], axis=0).astype(BF16)))
            (l_one, r_one), (l_two, r_two) = sides
            none = jnp.zeros_like(r_one)
            lhs = jnp.concatenate([l_one, l_two], axis=0)[:, :chan]
            rhs = jnp.concatenate([jnp.concatenate([r_one, none], axis=1),
                                   jnp.concatenate([none, r_two], axis=1)], axis=0)
            both = lax.dot_general(lhs, rhs, (((0,), (0,)), ((), ())), preferred_element_type=F32)
            x_ref[slot, q * chan:(q + 1) * chan, :] = both[:, :LANES]
            x_ref[slot, (q + 1) * chan:(q + 2) * chan, :] = both[:, LANES:]
        for j in range(chan // 2):
            even = x_ref[slot, pl.ds(2 * j, block, stride=chan), :]
            odd = x_ref[slot, pl.ds(2 * j + 1, block, stride=chan), :]
            lanes = slice(j * LANES, (j + 1) * LANES)
            out_ref[0, k, :, lanes] = jnp.where(low, even, roll_half(odd))
            out_ref[1, k, :, lanes] = jnp.where(low, roll_half(even), odd)


def whole(a):
    rank = a.ndim
    return pl.BlockSpec(a.shape, lambda i: (0,) * rank)


SMEM = pl.BlockSpec(memory_space=pltpu.SMEM)


def on_device(parts, inputs, cotangent, mode_weights, local_weight, local_bias):
    _, planes, grid, width = inputs.shape
    chan = local_weight.shape[0]
    pairs_here, zmodes, entries = mode_weights.shape[1:]
    pairs = pairs_here * parts
    half = grid // 2
    tab = np_tables(grid, zmodes)
    const = {name: jnp.asarray(t) for name, t in tab.items()}
    z_table = lax.dynamic_slice_in_dim(const["z_table"], lax.axis_index("mp") * planes, planes, 0)
    z_table = z_table.reshape(planes, 4 * zmodes)
    weights = jnp.transpose(mode_weights, (0, 2, 1, 3))
    params = pltpu.CompilerParams(**PARAMS)
    plane = pl.BlockSpec((1, 1, grid, width), lambda z: (0, z, 0, 0))
    flat = pl.BlockSpec((1, grid, width), lambda z: (z, 0, 0))
    modes_shape = jax.ShapeDtypeStruct((parts, zmodes, pairs_here, LANES), F32)
    modes_spec = pl.BlockSpec(modes_shape.shape, lambda z: (0, 0, 0, 0))
    acc = pltpu.VMEM((zmodes, pairs, LANES), F32)
    lines = pltpu.VMEM((4 * MX * half, LANES), F32)
    fy, iy, ix, twc, tws = (const[n] for n in ("fwd_y", "inv_y", "inv_x", "tw_c", "tw_s"))
    fx2, fx3 = const["fwd_x_two"], const["fwd_x_three"]

    def exchange(x):
        return lax.all_to_all(x, "mp", 0, 0)

    partial = pl.pallas_call(
        functools.partial(forward_kernel, zmodes, half),
        grid=(planes,),
        in_specs=[SMEM, plane, whole(fx2), whole(fy), whole(twc), whole(tws)],
        out_specs=modes_spec, out_shape=modes_shape, scratch_shapes=[acc, lines],
        compiler_params=params, name="forward",
    )(z_table, inputs, fx2, fy, twc, tws)

    block = 16
    w_spec = pl.BlockSpec((2, zmodes, block, entries), lambda i: (0, 0, i, 0))
    m_spec = pl.BlockSpec((zmodes, block, LANES), lambda i: (0, i, 0))
    many_spec = pl.BlockSpec((parts, zmodes, block, LANES), lambda i: (0, 0, i, 0))
    eye = np.eye(chan, dtype=np.float32)
    expand = np.concatenate([np.repeat(eye, chan, axis=1)] * 2, axis=0)
    fold = np.repeat(np.concatenate([eye, eye], axis=1), chan, axis=0)
    expand, fold = jnp.asarray(expand, BF16), jnp.asarray(fold, BF16)
    spectrum = jnp.sum(exchange(partial), axis=0)
    all_spectra = lax.all_gather(spectrum, "dp")
    mixed = pl.pallas_call(
        mix_kernel,
        grid=(pairs_here // block,),
        in_specs=[m_spec, w_spec, whole(expand)],
        out_specs=many_spec, out_shape=modes_shape,
        compiler_params=params, name="mix",
    )(spectrum, weights, expand)

    repeat = WIDE // chan
    eyes = jnp.eye(repeat, dtype=BF16)
    w_wide = jnp.kron(eyes, local_weight)
    wt_wide = jnp.kron(eyes, local_weight.T)
    bias = jnp.tile(local_bias, repeat)[None, :]
    outputs, slope, cot_partial = pl.pallas_call(
        functools.partial(middle_kernel, zmodes, half),
        grid=(planes,),
        in_specs=[SMEM, modes_spec, plane, plane, whole(w_wide), whole(bias), whole(iy), whole(ix),
                               whole(fx3), whole(fy), whole(twc), whole(tws)],
        out_specs=[plane, flat, modes_spec],
        out_shape=[jax.ShapeDtypeStruct(inputs.shape, BF16),
                   jax.ShapeDtypeStruct((planes, grid, width), F32), modes_shape],
        scratch_shapes=[acc, lines, lines, pltpu.VMEM((width // WIDE * grid, WIDE), F32)],
        compiler_params=params, name="middle",
    )(z_table, exchange(mixed), inputs, cotangent, w_wide, bias, iy, ix, fx3, fy, twc, tws)

    all_spectra, cot_partial = lax.optimization_barrier((all_spectra, cot_partial))
    cot_spectrum = jnp.sum(exchange(cot_partial), axis=0)
    all_cots = lax.all_gather(cot_spectrum, "dp")
    back = pl.pallas_call(
        back_kernel,
        grid=(pairs_here // block,),
        in_specs=[m_spec, w_spec, whole(fold)],
        out_specs=many_spec, out_shape=modes_shape,
        compiler_params=params, name="back",
    )(cot_spectrum, weights, fold)
    back_lines = exchange(back)

    input_grads = pl.pallas_call(
        functools.partial(final_kernel, zmodes, half),
        grid=(planes,),
        in_specs=[SMEM, modes_spec, flat, whole(wt_wide), whole(iy), whole(ix), whole(twc), whole(tws)],
        out_specs=plane, out_shape=jax.ShapeDtypeStruct(inputs.shape, BF16),
        scratch_shapes=[lines, pltpu.VMEM((2 * (width // WIDE) * grid, WIDE), F32)],
        compiler_params=params, name="final",
    )(z_table, back_lines, slope, wt_wide, iy, ix, twc, tws)

    all_cots, input_grads = lax.optimization_barrier((all_cots, input_grads))
    samples = all_spectra.shape[0]
    rows = samples * zmodes * pairs_here
    gathered = pl.BlockSpec((rows, LANES), lambda i: (0, 0))
    group = 8
    mode_grads = pl.pallas_call(
        functools.partial(grads_kernel, samples, pairs_here),
        grid=(pairs_here // group,),
        in_specs=[gathered, gathered],
        out_specs=pl.BlockSpec((2, zmodes, group, entries), lambda i: (0, 0, i, 0)),
        out_shape=jax.ShapeDtypeStruct((2, zmodes, pairs_here, entries), F32),
        scratch_shapes=[pltpu.VMEM((2, group * chan, LANES), F32)],
        cost_estimate=pl.CostEstimate(flops=2 * 2**30, bytes_accessed=2**26, transcendentals=0),
        compiler_params=params, name="grads",
    )(all_spectra.reshape(rows, LANES), all_cots.reshape(rows, LANES))
    mode_grads = jnp.transpose(mode_grads, (0, 2, 1, 3))
    return (outputs, input_grads, mode_grads)


def solution(mesh):
    field = P("dp", "mp", None, None)
    weights = P(None, "mp", None, None)
    return jax.shard_map(
        functools.partial(on_device, mesh.shape["mp"]),
        mesh=mesh,
        in_specs=(field, field, weights, P(), P()),
        out_specs=(field, field, weights),
        check_vma=False,
    )
```
